256 devices in a mesh: replica: 4 (over x_lo, core), shard: 64 (over x_hi, y, z).
Axes of the slice: x: 4 (x_hi: 2, x_lo: 2; x = x_hi * 2 + x_lo), y: 4, z: 8, core: 2. Of those that a mesh axis runs over, the one named last changes fastest.
Arguments:
- tokens: bfloat16 [65536, 18432], P(('replica', 'shard')), may hold values from -24 to 24
- cotangent: bfloat16 [65536, 256], P(('replica', 'shard')), may hold values from -6 to 6
- weight: bfloat16 [18432, 256], P('shard'), may hold values from -0.046875 to 0.046875
- moment_code: bfloat16 [18432, 256], P('shard'), may hold values from -1 to 1
- moment_scale: bfloat16 [18432, 2], P('shard'), may hold values from 0.29882812 to 3
- second_moment: bfloat16 [18432, 256], P('shard'), may hold values from 0.099609375 to 3
Outputs:
- outputs_next: bfloat16 [65536, 256], P(('replica', 'shard'))
- weight_new: bfloat16 [18432, 256], P('shard')
- code_new: bfloat16 [18432, 256], P('shard')
- scale_new: bfloat16 [18432, 2], P('shard')
- second_new: bfloat16 [18432, 256], P('shard')
The draws below stay inside these ranges and needn't reach their ends.
All inputs are finite; a program needn't handle non-finite values.
Results may differ from the reference program's by a relative error of at most 0.0049.
Values may be sent and summed in bfloat16 or wider, within the bound.
No kernel may reach another device: no remote copies, remote signals or barrier semaphores. Data moves between devices by JAX's collectives and lax.ppermute only.
A program may use at most 128 MiB of HBM per device.

```python
import math
import jax
import jax.numpy as jnp
from jax import lax

D = 18432
S = 256
HB = 128
TOK_DEV = 256
TOKENS = 65536
N_REPLICA = 4
N_SHARD = 64


def raised(values, stream_key, source, target, blocks, factor):
    def block_of(axis_at):
        return (jnp.arange(values.shape[axis_at]) // (values.shape[axis_at] // blocks)).reshape((-1,) + (1,) * (values.ndim - 1 - axis_at))

    one_side = jax.random.permutation(stream_key, blocks)[block_of(target)]
    other_side = (block_of(target) + blocks // 2) % blocks
    return jnp.where((block_of(source) == one_side) | (block_of(source) == other_side), factor * values, values)


def shard_levels(stream_key, extent, pieces, smallest, high):
    factor_of, own = 1.0, jax.random.fold_in(stream_key, 6)
    for position, blocks in pieces:
        draws = jnp.exp(jax.random.uniform(jax.random.fold_in(own, position), (blocks,), jnp.float32, smallest / len(pieces), high / len(pieces)))
        factor_of = factor_of * jnp.repeat(draws, extent[position] // blocks).reshape([-1 if axis == position else 1 for axis in range(len(extent))])
    return factor_of


def gaussian(stream_key, extent, width, most, cuts=(), held_as=jnp.bfloat16):
    array = jax.random.normal(stream_key, extent, jnp.float32) * width
    if len(cuts) > 0:
        array = shard_levels(stream_key, extent, cuts, -0.22, 0.18) * array
    return jnp.clip(array, min=-most, max=most).astype(held_as)


def noise_with(key, extent, deviation, bound, shards, heavy, held_as=jnp.bfloat16):
    drawn = deviation * jax.random.normal(key, extent, jnp.float32)
    if shards:
        drawn = drawn * shard_levels(key, extent, shards, -0.22, 0.18)
    return jnp.clip(raised(drawn, jax.random.fold_in(key, 3), *heavy), -bound, bound).astype(held_as)


def setup_inputs(seed: int = 0) -> dict:
    seeds = jax.random.split(jax.random.key(seed), 7)
    tokens = noise_with(seeds[0], (TOKENS, D), 1.0, 24.0, ((0, 256),), (0, 1, 256, 6.0))
    cotangent = gaussian(seeds[1], (TOKENS, S), 1.0, 6.0, ((0, 256),))
    weight = gaussian(seeds[2], (D, S), D ** -0.5, 0.046875, ((0, 64),))
    moment_code = jnp.clip(jax.random.uniform(seeds[3], (D, S), jnp.float32, -1.0, 1.0) * shard_levels(seeds[3], (D, S), ((0, 64),), -0.4, 0.0), -1.0, 1.0).astype(jnp.bfloat16)
    moment_scale = jnp.clip(jnp.exp(math.log(3.0) - 2.306499 * jax.random.uniform(seeds[4], (D, S // HB), jnp.float32) ** shard_levels(seeds[4], (D, S // HB), ((0, 64),), -0.2, 0.2)), 0.29882812, 3.0).astype(jnp.bfloat16)
    second_moment = jnp.clip(jnp.exp(math.log(3.0) - 3.4051113 * jax.random.uniform(seeds[5], (D, S), jnp.float32) ** shard_levels(seeds[5], (D, S), ((0, 64),), -0.2, 0.2)), 0.099609375, 3.0).astype(jnp.bfloat16)
    return {"tokens": tokens, "cotangent": cotangent, "weight": weight, "moment_code": moment_code, "moment_scale": moment_scale, "second_moment": second_moment}


def hadamard_table():
    index = jnp.arange(128, dtype=jnp.int32)
    parity = jnp.zeros((128, 128), jnp.int32)
    for level in range(7):
        left = jnp.bitwise_and(jnp.right_shift(index, level), 1)
        parity = parity + left[:, None] * left[None, :]
    signs = 1 - 2 * jnp.bitwise_and(parity, 1)
    return signs.astype(jnp.float32) / math.sqrt(128.0)

def adam_rows(grad, weight, code, scale, second_old):
    rows, cols = grad.shape
    blocks = cols // 128
    table = hadamard_table()
    stored = code.astype(jnp.float32).reshape(rows, blocks, 128) * scale.astype(jnp.float32)[:, :, None]
    first_old = jnp.einsum('rbk,kj->rbj', stored, table, precision=lax.Precision.HIGHEST).reshape(rows, cols)
    first = 0.9 * first_old + 0.1 * grad
    second = 0.95 * second_old.astype(jnp.float32) + 0.05 * grad * grad
    weight_new = (weight.astype(jnp.float32) - 0.002 * first / (jnp.sqrt(second) + 1e-08)).astype(jnp.bfloat16)
    rotated = jnp.einsum('rbk,kj->rbj', first.reshape(rows, blocks, 128), table, precision=lax.Precision.HIGHEST)
    scale_new = lax.optimization_barrier(jnp.max(jnp.abs(rotated), axis=2)).astype(jnp.bfloat16)
    scale_back = lax.optimization_barrier(scale_new).astype(jnp.float32)
    code_new = (rotated / (scale_back[:, :, None] + 1e-06)).reshape(rows, cols).astype(jnp.bfloat16)
    return (weight_new, code_new, scale_new, second.astype(jnp.bfloat16))

def reference(tokens, cotangent, weight, moment_code, moment_scale, second_moment):
    count = N_REPLICA * N_SHARD
    token_blocks = tokens.reshape(count, TOK_DEV, D)
    cot_blocks = cotangent.reshape(count, TOK_DEV, S)

    def accumulate(total, pair):
        return (total + jnp.dot(pair[0].T, pair[1], preferred_element_type=jnp.float32), None)
    summed, unused = lax.scan(accumulate, jnp.zeros((D, S), jnp.float32), (token_blocks, cot_blocks))
    grad = summed / math.sqrt(TOKENS)
    weight_new, code_new, scale_new, second_new = adam_rows(grad, weight, moment_code, moment_scale, second_moment)
    outputs_next = lax.map(lambda block: jnp.dot(block, weight_new, preferred_element_type=jnp.float32).astype(jnp.bfloat16), token_blocks)
    return (outputs_next.reshape(TOKENS, S), weight_new, code_new, scale_new, second_new)
```

```python
import math

import jax
import jax.numpy as jnp
from jax import lax
from jax.sharding import Mesh, PartitionSpec as P

AXES = ("xl", "c", "xh", "y", "z")
X = ("xl", "xh")
HALF = 9216
BF = jnp.bfloat16
F32 = jnp.float32


def x_pairs(step):
    where = lambda x: (x % 2) * 2 + x // 2
    return [(where(i), where((i + step) % 4)) for i in range(4)]


def y_pairs(step):
    return [(i, (i + step) % 4) for i in range(4)]


SWAP = [(0, 1), (1, 0)]


def hadamard_table():
    index = jnp.arange(128, dtype=jnp.int32)
    parity = jnp.zeros((128, 128), jnp.int32)
    for level in range(7):
        left = jnp.bitwise_and(jnp.right_shift(index, level), 1)
        parity = parity + left[:, None] * left[None, :]
    signs = 1 - 2 * jnp.bitwise_and(parity, 1)
    return signs.astype(F32) / math.sqrt(128.0)


def rotate(values, table):
    return jnp.einsum("brk,kj->brj", values, table, precision=lax.Precision.HIGHEST)


def adam(grad, weight, code, scale, second_old):
    table = hadamard_table()
    first_old = rotate(code.astype(F32) * scale.astype(F32), table)
    first = 0.9 * first_old + 0.1 * grad
    second = 0.95 * second_old.astype(F32) + 0.05 * grad * grad
    weight_new = (weight.astype(F32) - 0.002 * first / (jnp.sqrt(second) + 1e-08)).astype(BF)
    rotated = rotate(first, table)
    scale_new = jnp.max(jnp.abs(rotated), axis=2, keepdims=True).astype(BF)
    scale_back = lax.optimization_barrier(scale_new).astype(F32)
    code_new = (rotated / (scale_back + 1e-06)).astype(BF)
    return weight_new, code_new, scale_new, second.astype(BF)


def at(array, index, axis):
    return lax.dynamic_index_in_dim(array, index, axis, keepdims=False)


def per_device(tokens, cotangent, weight, code, scale, second_old):
    c = lax.axis_index("c")
    xh = lax.axis_index("xh")
    x = xh * 2 + lax.axis_index("xl")
    y = lax.axis_index("y")

    state = jnp.concatenate([weight, code, second_old, jnp.pad(scale, ((0, 0), (0, 126)))], axis=1)
    state = state.reshape(4, 72, 896)
    got = lax.ppermute(at(state, (x + 2) % 4, 0), "xh", SWAP)
    mine = jnp.where(xh == c, at(state, x, 0), got)

    def blocks(array):
        return array.reshape(72, 2, 128).transpose(1, 0, 2)

    weight_m = blocks(mine[:, :256])
    code_m = blocks(mine[:, 256:512])
    second_m = blocks(mine[:, 512:768])
    scale_m = mine[:, 768:770].T[:, :, None]

    own = lax.dynamic_slice(tokens, (0, c * HALF), (256, HALF))
    other = lax.ppermute(lax.dynamic_slice(tokens, (0, (1 - c) * HALF), (256, HALF)), "c", SWAP)
    cot_other = lax.ppermute(cotangent, "c", SWAP)
    contract = (((0,), (0,)), ((), ()))
    grad = lax.dot_general(own, cotangent, contract, preferred_element_type=F32)
    grad = grad + lax.dot_general(other, cot_other, contract, preferred_element_type=F32)
    grad = grad.reshape(4, 8, 4, 72, 256)

    def reduce_over(term, axis, pairs, place, dim):
        sent = term.astype(BF)
        total = at(term, place, dim)
        for step in (2, 1, 3):
            total = total + lax.ppermute(at(sent, (place + step) % 4, dim), axis, pairs(step)).astype(F32)
        return total

    a = reduce_over(grad[..., :128], X, x_pairs, x, 2)
    b = reduce_over(grad[..., 128:], "y", y_pairs, y, 0)
    a = reduce_over(a, "y", y_pairs, y, 0)
    b = reduce_over(b, X, x_pairs, x, 1)
    ab = lax.all_to_all(jnp.stack([a, b], axis=1), "z", 0, 0, tiled=True)
    grad_m = jnp.sum(ab, axis=0) * (1.0 / 256.0)

    weight_new, code_new, scale_new, second_new = adam(grad_m, weight_m, code_m, scale_m, second_m)

    def rows(array):
        return array.transpose(1, 0, 2).reshape(72, 256)

    def gather(block, axis, pairs, place, dim):
        parts = [block] + [lax.ppermute(block, axis, pairs(step)) for step in (3, 2, 1)]
        twice = jnp.stack(parts + parts, axis=dim)
        return lax.dynamic_slice_in_dim(twice, (4 - place) % 4, 4, dim)

    made = jnp.concatenate(
        [rows(weight_new), rows(code_new), rows(second_new), jnp.pad(scale_new[:, :, 0].T, ((0, 0), (0, 126)))], axis=1
    )
    made = gather(made, X, x_pairs, x, 0)
    made = jnp.where(xh == c, made, lax.ppermute(made, "c", SWAP)).reshape(288, 896)

    ab = lax.all_to_all(jnp.broadcast_to(weight_new[None], (8, 2, 72, 128)), "z", 0, 0, tiled=True)
    a = gather(ab[:, 0], "y", y_pairs, y, 0)
    b = gather(ab[:, 1], X, x_pairs, x, 1)
    a = gather(a, X, x_pairs, x, 2).reshape(HALF, 128)
    b = gather(b, "y", y_pairs, y, 0).reshape(HALF, 128)
    slab = jnp.concatenate([a, b], axis=1)
    part_other = lax.ppermute(jnp.dot(other, slab, preferred_element_type=F32), "c", SWAP)
    outputs = jnp.dot(own, slab, preferred_element_type=F32) + part_other
    return (outputs.astype(BF), made[:, :256], made[:, 256:512], made[:, 768:770], made[:, 512:768])


def solution(mesh):
    split = Mesh(mesh.devices.reshape(2, 2, 2, 4, 8), AXES)
    tokens = P(AXES, None)
    shard = P(("xh", "y", "z"), None)
    return jax.shard_map(
        per_device,
        mesh=split,
        in_specs=(tokens, tokens, shard, shard, shard, shard),
        out_specs=(tokens, shard, shard, shard, shard),
        check_vma=False,
    )
```

```python
import itertools
import math

import jax
import jax.numpy as jnp
from jax import lax
from jax.experimental import pallas as pl
from jax.experimental.pallas import tpu as pltpu
from jax.sharding import Mesh, PartitionSpec as P

AXES = ("xl", "c", "xh", "y", "z")
PLANE = ("xl", "c", "xh", "y")
BF = jnp.bfloat16
F32 = jnp.float32
SWAP = [(0, 1), (1, 0)]


def flat(x, c, y):
    return ((x % 2 * 2 + c) * 2 + x // 2) * 4 + y


def line_pairs(first, step):
    pairs = []
    for x in range(4):
        for c in range(2):
            for y in range(4):
                along_x = (c == 0) == first
                to = flat((x + step) % 4, c, y) if along_x else flat(x, c, (y + step) % 4)
                pairs.append((flat(x, c, y), to))
    return pairs


def home_pairs():
    pairs = []
    for c in range(2):
        for p in range(4):
            owners = [(p, c, q) if c == 0 else (q, c, p) for q in range(4)]
            holders = [(2 * c + i, core, p) for i in range(2) for core in range(2)]

            def hops(order):
                apart = lambda a, b: min((a - b) % 4, (b - a) % 4)
                pair = zip(owners, order)
                each = [apart(o[0], h[0]) + apart(o[2], h[2]) + (0.1 if o[1] != h[1] else 0) for o, h in pair]
                return sum(each) + 0.01 * max(each)

            best = min(itertools.permutations(holders), key=hops)
            pairs += [(flat(*owners[q]), flat(*best[q]), q) for q in range(4)]
    return pairs


def hadamard_table():
    index = jnp.arange(128, dtype=jnp.int32)
    parity = jnp.zeros((128, 128), jnp.int32)
    for level in range(7):
        left = jnp.bitwise_and(jnp.right_shift(index, level), 1)
        parity = parity + left[:, None] * left[None, :]
    signs = 1 - 2 * jnp.bitwise_and(parity, 1)
    return signs.astype(F32) / math.sqrt(128.0)


def call(kernel, out_shape, scratch=(), in_specs=None):
    options = {} if in_specs is None else {"in_specs": in_specs}
    return pl.pallas_call(
        kernel,
        out_shape=out_shape,
        scratch_shapes=scratch,
        compiler_params=pltpu.CompilerParams(vmem_limit_bytes=16 << 20),
        cost_estimate=pl.CostEstimate(flops=1000, bytes_accessed=1000, transcendentals=0),
        **options,
    )


def shaped(shape, dtype):
    return jax.ShapeDtypeStruct(shape, dtype)


def after(value, *others):
    return lax.optimization_barrier((value, *others))[0]


SCALAR = pl.BlockSpec(memory_space=pltpu.SMEM)
VMEM = pl.BlockSpec(memory_space=pltpu.VMEM)


def gradient_rows(own, other, cot_own, cot_other, rows, dtype, added=()):
    contract = (((0,), (0,)), ((), ()))
    size = rows.stop - rows.start

    def kernel(own_ref, other_ref, cot_own_ref, cot_other_ref, *refs):
        for i in range(0, size, 384):
            part = pl.ds(rows.start + i, 384)
            term = lax.dot_general(own_ref[:, part], cot_own_ref[...], contract, preferred_element_type=F32)
            term += lax.dot_general(other_ref[:, part], cot_other_ref[...], contract, preferred_element_type=F32)
            for ref in refs[:-1]:
                term += ref[pl.ds(i, 384), :].astype(F32)
            refs[-1][pl.ds(i, 384), :] = term.astype(dtype)

    return call(kernel, shaped((size, 256), dtype))(own, other, cot_own, cot_other, *added)


def sum_and_split(total, upper, lower, q):
    def kernel(q_ref, total_ref, a_ref, b_ref, d_ref, e_ref, keep_ref, one_ref, two_ref, three_ref, value_ref):
        for z in range(8):
            rows, local = pl.ds(z * 288, 288), pl.ds(z % 4 * 288, 288)
            f_ref, g_ref = (a_ref, b_ref) if z < 4 else (d_ref, e_ref)
            value_ref[rows, :] = total_ref[rows, :] + f_ref[local, :].astype(F32) + g_ref[local, :].astype(F32)
            for step, ref in enumerate((keep_ref, one_ref, two_ref, three_ref)):
                at = pl.multiple_of(z * 288 + (q_ref[0] + step) % 4 * 72, 8)
                ref[z] = value_ref[pl.ds(at, 72), :].astype(ref.dtype)

    return call(
        kernel,
        [shaped((8, 72, 256), F32)] + [shaped((8, 72, 256), BF)] * 3,
        [pltpu.VMEM((2304, 256), F32)],
        [SCALAR] + [VMEM] * 5,
    )(q.reshape(1), total, *upper, *lower)


def sum_rows(keep, terms):
    def kernel(keep_ref, a_ref, b_ref, d_ref, out_ref):
        out_ref[...] = (
            keep_ref[...] + a_ref[...].astype(F32) + b_ref[...].astype(F32) + d_ref[...].astype(F32)
        ).astype(BF)

    return call(kernel, shaped((8, 72, 256), BF))(keep, *terms)


def adam(terms, state, table):
    def kernel(terms_ref, state_ref, table_ref, copies_ref, made_ref):
        grad = terms_ref[0].astype(F32)
        for z in range(1, 8):
            grad += terms_ref[z].astype(F32)
        grad *= 1.0 / 256.0
        table = table_ref[...]

        def rotate(block):
            return jnp.dot(block, table, precision=lax.Precision.HIGHEST, preferred_element_type=F32)

        second = 0.95 * state_ref[2].astype(F32) + 0.05 * grad * grad
        code = state_ref[1].astype(F32)
        weight = state_ref[0].astype(F32)
        scale = state_ref[3].astype(F32)
        scales = []
        for block in range(2):
            at = slice(128 * block, 128 * block + 128)
            first_old = rotate(code[:, at] * scale[:, block : block + 1])
            first = 0.9 * first_old + 0.1 * grad[:, at]
            weight_new = (weight[:, at] - 0.002 * first / (jnp.sqrt(second[:, at]) + 1e-08)).astype(BF)
            for z in range(8):
                copies_ref[z, :, at] = weight_new
            rotated = rotate(first)
            scales.append(jnp.max(jnp.abs(rotated), axis=1, keepdims=True).astype(BF).astype(F32))
            made_ref[0, :, at] = (rotated / (scales[block] + 1e-06)).astype(BF)
        made_ref[1] = second.astype(BF)
        column = lax.broadcasted_iota(jnp.int32, (72, 256), 1)
        made_ref[2] = jnp.where(column % 2 == 0, scales[0], scales[1]).astype(BF)

    return call(kernel, [shaped((8, 72, 256), BF), shaped((3, 72, 256), BF)])(terms, state, table)


def both_cores(*arrays):
    part = sum(a.reshape(-1, 256)[:16, :128] for a in arrays)
    return lax.ppermute(part, "c", SWAP)


def join(parts, q, z, ready):
    def kernel(place_ref, a_ref, b_ref, d_ref, e_ref, ready_ref, upper_ref, lower_ref, home_ref):
        column = lax.broadcasted_iota(jnp.int32, (72, 256), 1)
        scales = jnp.zeros((72, 256), F32)
        for step, ref in enumerate((a_ref, b_ref, d_ref, e_ref)):
            quarter = (place_ref[0] + step) % 4
            upper_ref[:, quarter] = ref[:4]
            lower_ref[:, quarter] = ref[4:8]
            home_ref[quarter] = ref[place_ref[1]]
            home_ref[4 + quarter] = ref[8]
            home_ref[8 + quarter] = ref[9]
            scales = jnp.where(column // 2 == quarter, ref[10].astype(F32), scales)
        home_ref[12] = scales.astype(BF)

    return call(
        kernel,
        [shaped((4, 4, 72, 256), BF)] * 2 + [shaped((13, 72, 256), BF)],
        (),
        [SCALAR] + [VMEM] * 5,
    )(jnp.stack([q, z]), *parts, ready)


def unpack(home):
    def kernel(home_ref, weight_ref, code_ref, second_ref, scale_ref):
        weight_ref[...] = home_ref[:4]
        code_ref[...] = home_ref[4:8]
        second_ref[...] = home_ref[8:12]
        for quarter in range(4):
            scale_ref[quarter] = home_ref[12][:, 2 * quarter : 2 * quarter + 2]

    return call(kernel, [shaped((4, 72, 256), BF)] * 3 + [shaped((4, 72, 2), BF)])(home)


def outputs_chunk(own, other, upper, lower, total):
    def kernel(own_ref, other_ref, upper_ref, lower_ref, *refs):
        for half, ref in ((slice(0, 256), own_ref), (slice(256, 512), other_ref)):
            value = jnp.dot(ref[:, :1152], upper_ref[...], preferred_element_type=F32)
            value += jnp.dot(ref[:, 1152:], lower_ref[...], preferred_element_type=F32)
            refs[-1][half] = value if total is None else refs[0][half] + value

    given = [] if total is None else [total]
    return call(kernel, shaped((512, 256), F32))(own, other, upper, lower, *given)


def per_device(tokens, cotangent, weight, code, scale, second_old):
    xl = lax.axis_index("xl")
    c = lax.axis_index("c")
    x = lax.axis_index("xh") * 2 + xl
    y = lax.axis_index("y")
    p = jnp.where(c == 0, x, y)
    q = jnp.where(c == 0, y, x)

    home = home_pairs()

    def taken(place, *behind):
        return lax.dynamic_slice(tokens, (0, after(place, *behind) * 2304), (256, 2304))

    def sent(step, *behind):
        return taken((1 - c) * 4 + (q + step) % 4, *behind)

    def kept(step, *behind):
        return taken(c * 4 + (p + step) % 4, *behind)

    def swap(chunk):
        return lax.ppermute(chunk, "c", SWAP)

    def pass_on(rows, step):
        return lax.ppermute(rows, PLANE, line_pairs(True, step))

    def rows_of(step, rows, *added, dtype=BF):
        return gradient_rows(own[step], other[step], cotangent, cot_other, rows, dtype, added)

    upper, lower, both = slice(0, 1152), slice(1152, 2304), slice(0, 2304)
    own, other = {}, {}
    cot_other = swap(cotangent)
    chunk = sent(2)
    other[2] = swap(after(chunk, cot_other))
    quarter = [0] * 32
    for _, holder, which in home:
        quarter[holder] = which
    here = ((xl * 2 + c) * 2 + lax.axis_index("xh")) * 4 + y
    at = after(jnp.asarray(quarter, jnp.int32)[here], chunk) * 72
    state = [weight, code, second_old, jnp.pad(scale, ((0, 0), (0, 254)))]
    state = jnp.stack([lax.dynamic_slice(a, (at, 0), (72, 256)) for a in state])
    state = lax.ppermute(state, PLANE, [(b, a) for a, b, _ in home])
    taken_here = [kept(step, chunk) for step in (2, 1, 3, 0)]
    taken_there = [sent(step, chunk) for step in (1, 3, 0)]
    *taken_here, one, three, zero = lax.optimization_barrier((*taken_here, *taken_there))
    own = dict(zip((2, 1, 3, 0), taken_here))
    other[1], other[3], other[0] = swap(one), swap(three), swap(zero)
    from_left, from_right = pass_on(rows_of(2, upper), 1), pass_on(rows_of(2, lower), 3)
    own[1] = after(own[1], state)
    left_lower = pass_on(rows_of(1, lower), 1)
    right_upper = pass_on(rows_of(3, upper), 3)
    left_upper = pass_on(rows_of(1, upper, from_left), 1)
    right_lower = pass_on(rows_of(3, lower, from_right), 3)
    total = rows_of(0, both, dtype=F32)

    keep, *pieces = sum_and_split(total, (left_upper, right_upper), (left_lower, right_lower), q)
    got = [lax.ppermute(pieces[step - 1], PLANE, line_pairs(False, step)) for step in (1, 3, 2)]
    grad = lax.all_to_all(sum_rows(keep, got), "z", 0, 0, tiled=True)
    copies, made = adam(grad, state, hadamard_table())

    slab = lax.all_to_all(copies, "z", 0, 0, tiled=True)
    slab = jnp.concatenate([slab, made])
    got = {step: lax.ppermute(slab, PLANE, line_pairs(False, step)) for step in (1, 3, 2)}
    upper, lower, made = join([slab, got[3], got[2], got[1]], q, lax.axis_index("z"), both_cores(*got.values()))
    upper, lower = upper.reshape(1152, 256), lower.reshape(1152, 256)
    left_upper, right_lower = pass_on(upper, 1), pass_on(lower, 3)
    left_lower, right_upper = pass_on(lower, 1), pass_on(upper, 3)

    for step in range(4):
        own[step] = kept(step, copies)
    out = outputs_chunk(own[0], other[0], upper, lower, None)
    made = lax.ppermute(after(made, out), PLANE, [(a, b) for a, b, _ in home])
    upper, lower = pass_on(left_upper, 1), pass_on(right_lower, 3)
    out = outputs_chunk(own[3], other[3], left_upper, left_lower, out)
    out = outputs_chunk(own[1], other[1], right_upper, right_lower, out)
    out = outputs_chunk(own[2], other[2], upper, lower, out)
    weight_new, code_new, second_new, scale_new = unpack(made)
    outputs = (out[:256] + lax.ppermute(out[256:], "c", SWAP)).astype(BF)
    rows = lambda a: a.reshape(288, a.shape[2])
    return (outputs, rows(weight_new), rows(code_new), rows(scale_new), rows(second_new))


def solution(mesh):
    split = Mesh(mesh.devices.reshape(2, 2, 2, 4, 8), AXES)
    tokens = P(AXES, None)
    shard = P(("xh", "y", "z"), None)
    return jax.shard_map(
        per_device,
        mesh=split,
        in_specs=(tokens, tokens, shard, shard, shard, shard),
        out_specs=(tokens, shard, shard, shard, shard),
        check_vma=False,
    )
```

```python
import itertools
import math

import jax
import jax.numpy as jnp
from jax import lax
from jax.experimental import pallas as pl
from jax.experimental.pallas import tpu as pltpu
from jax.sharding import Mesh, PartitionSpec as P

AXES = ("xl", "c", "xh", "y", "z")
PLANE = ("xl", "c", "xh", "y")
BF = jnp.bfloat16
F32 = jnp.float32
SWAP = [(0, 1), (1, 0)]


def flat(x, c, y):
    return ((x % 2 * 2 + c) * 2 + x // 2) * 4 + y


def line_pairs(first, step):
    pairs = []
    for x in range(4):
        for c in range(2):
            for y in range(4):
                along_x = (c == 0) == first
                to = flat((x + step) % 4, c, y) if along_x else flat(x, c, (y + step) % 4)
                pairs.append((flat(x, c, y), to))
    return pairs


def home_pairs():
    pairs = []
    for c in range(2):
        for p in range(4):
            owners = [(p, c, q) if c == 0 else (q, c, p) for q in range(4)]
            holders = [(2 * c + i, core, p) for i in range(2) for core in range(2)]

            def hops(order):
                apart = lambda a, b: min((a - b) % 4, (b - a) % 4)
                pair = zip(owners, order)
                each = [apart(o[0], h[0]) + apart(o[2], h[2]) + (0.1 if o[1] != h[1] else 0) for o, h in pair]
                return sum(each) + 0.01 * max(each)

            best = min(itertools.permutations(holders), key=hops)
            pairs += [(flat(*owners[q]), flat(*best[q]), q) for q in range(4)]
    return pairs


def hadamard_table():
    index = jnp.arange(128, dtype=jnp.int32)
    parity = jnp.zeros((128, 128), jnp.int32)
    for level in range(7):
        left = jnp.bitwise_and(jnp.right_shift(index, level), 1)
        parity = parity + left[:, None] * left[None, :]
    signs = 1 - 2 * jnp.bitwise_and(parity, 1)
    return signs.astype(F32) / math.sqrt(128.0)


def call(kernel, out_shape, scratch=(), in_specs=None):
    options = {} if in_specs is None else {"in_specs": in_specs}
    return pl.pallas_call(
        kernel,
        out_shape=out_shape,
        scratch_shapes=scratch,
        compiler_params=pltpu.CompilerParams(vmem_limit_bytes=16 << 20),
        cost_estimate=pl.CostEstimate(flops=1000, bytes_accessed=1000, transcendentals=0),
        **options,
    )


def shaped(shape, dtype):
    return jax.ShapeDtypeStruct(shape, dtype)


def after(value, *others):
    return lax.optimization_barrier((value, *others))[0]


SCALAR = pl.BlockSpec(memory_space=pltpu.SMEM)
VMEM = pl.BlockSpec(memory_space=pltpu.VMEM)
ANY = pl.BlockSpec(memory_space=pl.ANY)


def gradient_rows(own, other, cot_own, cot_other, rows, dtype, added=(), behind=()):
    contract = (((0,), (0,)), ((), ()))
    size = rows.stop - rows.start

    def kernel(own_ref, other_ref, cot_own_ref, cot_other_ref, *refs):
        for i in range(0, size, 384):
            part = pl.ds(rows.start + i, 384)
            term = lax.dot_general(own_ref[:, part], cot_own_ref[...], contract, preferred_element_type=F32)
            term += lax.dot_general(other_ref[:, part], cot_other_ref[...], contract, preferred_element_type=F32)
            for ref in refs[: len(added)]:
                term += ref[pl.ds(i, 384), :].astype(F32)
            refs[-1][pl.ds(i, 384), :] = term.astype(dtype)

    specs = [VMEM] * (4 + len(added)) + [ANY] * len(behind)
    return call(kernel, shaped((size, 256), dtype), (), specs)(own, other, cot_own, cot_other, *added, *behind)


def sum_and_split(total, upper, lower, q):
    def kernel(q_ref, total_ref, a_ref, b_ref, d_ref, e_ref, keep_ref, one_ref, two_ref, three_ref, value_ref):
        for z in range(8):
            rows, local = pl.ds(z * 288, 288), pl.ds(z % 4 * 288, 288)
            f_ref, g_ref = (a_ref, b_ref) if z < 4 else (d_ref, e_ref)
            value_ref[rows, :] = total_ref[rows, :] + f_ref[local, :].astype(F32) + g_ref[local, :].astype(F32)
            for step, ref in enumerate((keep_ref, one_ref, two_ref, three_ref)):
                at = pl.multiple_of(z * 288 + (q_ref[0] + step) % 4 * 72, 8)
                ref[z] = value_ref[pl.ds(at, 72), :].astype(ref.dtype)

    return call(
        kernel,
        [shaped((8, 72, 256), F32)] + [shaped((8, 72, 256), BF)] * 3,
        [pltpu.VMEM((2304, 256), F32)],
        [SCALAR] + [VMEM] * 5,
    )(q.reshape(1), total, *upper, *lower)


def sum_rows(keep, terms):
    def kernel(keep_ref, a_ref, b_ref, d_ref, out_ref):
        out_ref[...] = (
            keep_ref[...] + a_ref[...].astype(F32) + b_ref[...].astype(F32) + d_ref[...].astype(F32)
        ).astype(BF)

    return call(kernel, shaped((8, 72, 256), BF))(keep, *terms)


def adam(terms, state, table):
    def kernel(terms_ref, state_ref, table_ref, copies_ref, made_ref):
        grad = terms_ref[0].astype(F32)
        for z in range(1, 8):
            grad += terms_ref[z].astype(F32)
        grad *= 1.0 / 256.0
        table = table_ref[...]

        def rotate(block):
            return jnp.dot(block, table, precision=lax.Precision.HIGHEST, preferred_element_type=F32)

        second = 0.95 * state_ref[2].astype(F32) + 0.05 * grad * grad
        code = state_ref[1].astype(F32)
        weight = state_ref[0].astype(F32)
        scale = state_ref[3].astype(F32)
        scales = []
        for block in range(2):
            at = slice(128 * block, 128 * block + 128)
            first_old = rotate(code[:, at] * scale[:, block : block + 1])
            first = 0.9 * first_old + 0.1 * grad[:, at]
            weight_new = (weight[:, at] - 0.002 * first / (jnp.sqrt(second[:, at]) + 1e-08)).astype(BF)
            for z in range(8):
                copies_ref[z, :, at] = weight_new
            rotated = rotate(first)
            scales.append(jnp.max(jnp.abs(rotated), axis=1, keepdims=True).astype(BF).astype(F32))
            made_ref[0, :, at] = (rotated / (scales[block] + 1e-06)).astype(BF)
        made_ref[1] = second.astype(BF)
        column = lax.broadcasted_iota(jnp.int32, (72, 256), 1)
        made_ref[2] = jnp.where(column % 2 == 0, scales[0], scales[1]).astype(BF)

    return call(kernel, [shaped((8, 72, 256), BF), shaped((3, 72, 256), BF)])(terms, state, table)


def stacked(slab, made):
    def kernel(slab_ref, made_ref, out_ref):
        out_ref[:8] = slab_ref[...]
        out_ref[8:] = made_ref[...]

    return call(kernel, shaped((11, 72, 256), BF))(slab, made)


def both_cores(*arrays):
    def kernel(*refs):
        refs[-1][...] = jnp.zeros((16, 128), BF)

    return lax.ppermute(call(kernel, shaped((16, 128), BF), (), [ANY] * len(arrays))(*arrays), "c", SWAP)


def join(parts, q, z, ready):
    def kernel(place_ref, a_ref, b_ref, d_ref, e_ref, ready_ref, upper_ref, lower_ref, home_ref):
        column = lax.broadcasted_iota(jnp.int32, (72, 256), 1)
        scales = jnp.zeros((72, 256), F32)
        for step, ref in enumerate((a_ref, b_ref, d_ref, e_ref)):
            quarter = (place_ref[0] + step) % 4
            upper_ref[:, quarter] = ref[:4]
            lower_ref[:, quarter] = ref[4:8]
            home_ref[quarter] = ref[place_ref[1]]
            home_ref[4 + quarter] = ref[8]
            home_ref[8 + quarter] = ref[9]
            scales = jnp.where(column // 2 == quarter, ref[10].astype(F32), scales)
        home_ref[12] = scales.astype(BF)

    return call(
        kernel,
        [shaped((4, 4, 72, 256), BF)] * 2 + [shaped((13, 72, 256), BF)],
        (),
        [SCALAR] + [VMEM] * 4 + [ANY],
    )(jnp.stack([q, z]), *parts, ready)


def unpack(home):
    def kernel(home_ref, weight_ref, code_ref, second_ref, scale_ref):
        weight_ref[...] = home_ref[:4]
        code_ref[...] = home_ref[4:8]
        second_ref[...] = home_ref[8:12]
        for quarter in range(4):
            scale_ref[quarter] = home_ref[12][:, 2 * quarter : 2 * quarter + 2]

    return call(kernel, [shaped((4, 72, 256), BF)] * 3 + [shaped((4, 72, 2), BF)])(home)


def outputs_chunk(own, other, upper, lower, total):
    def kernel(own_ref, other_ref, upper_ref, lower_ref, *refs):
        for half, ref in ((slice(0, 256), own_ref), (slice(256, 512), other_ref)):
            value = jnp.dot(ref[:, :1152], upper_ref[...], preferred_element_type=F32)
            value += jnp.dot(ref[:, 1152:], lower_ref[...], preferred_element_type=F32)
            refs[-1][half] = value if total is None else refs[0][half] + value

    given = [] if total is None else [total]
    return call(kernel, shaped((512, 256), F32))(own, other, upper, lower, *given)


def per_device(tokens, cotangent, weight, code, scale, second_old):
    xl = lax.axis_index("xl")
    c = lax.axis_index("c")
    x = lax.axis_index("xh") * 2 + xl
    y = lax.axis_index("y")
    p = jnp.where(c == 0, x, y)
    q = jnp.where(c == 0, y, x)

    home = home_pairs()

    def taken(place, *behind):
        return lax.dynamic_slice(tokens, (0, after(place, *behind) * 2304), (256, 2304))

    def sent(step, *behind):
        return taken((1 - c) * 4 + (q + step) % 4, *behind)

    def kept(step, *behind):
        return taken(c * 4 + (p + step) % 4, *behind)

    def swap(chunk):
        return lax.ppermute(chunk, "c", SWAP)

    def pass_on(rows, step):
        return lax.ppermute(rows, PLANE, line_pairs(True, step))

    def rows_of(step, rows, *added, dtype=BF, behind=()):
        return gradient_rows(own[step], other[step], cotangent, cot_other, rows, dtype, added, behind)

    upper, lower, both = slice(0, 1152), slice(1152, 2304), slice(0, 2304)
    own, other = {}, {}
    cot_other = swap(cotangent)
    chunk = sent(2)
    other[2] = swap(after(chunk, cot_other))
    words = [0] * 4
    for _, holder, which in home:
        words[holder // 8] += which << (holder % 8 * 2)
    word = jnp.where(xl == 0, jnp.where(c == 0, words[0], words[1]), jnp.where(c == 0, words[2], words[3]))
    at = lax.shift_right_logical(word, 2 * (lax.axis_index("xh") * 4 + y)) % 4
    at = after(at, chunk) * 72
    state = [weight, code, second_old, jnp.pad(scale, ((0, 0), (0, 254)))]
    state = jnp.stack([lax.dynamic_slice(a, (at, 0), (72, 256)) for a in state])
    state = lax.ppermute(state, PLANE, [(b, a) for a, b, _ in home])
    taken_here = [kept(step, chunk) for step in (2, 1, 3, 0)]
    taken_there = [sent(step, chunk) for step in (1, 3, 0)]
    *taken_here, one, three, zero = lax.optimization_barrier((*taken_here, *taken_there))
    own = dict(zip((2, 1, 3, 0), taken_here))
    other[1], other[3], other[0] = swap(one), swap(three), swap(zero)
    from_left, from_right = pass_on(rows_of(2, upper), 1), pass_on(rows_of(2, lower), 3)
    left_lower = pass_on(rows_of(1, lower), 1)
    right_upper = pass_on(rows_of(3, upper), 3)
    left_upper = pass_on(rows_of(1, upper, from_left), 1)
    right_lower = pass_on(rows_of(3, lower, from_right), 3)
    total = rows_of(0, both, dtype=F32, behind=(state,))

    keep, *pieces = sum_and_split(total, (left_upper, right_upper), (left_lower, right_lower), q)
    got = [lax.ppermute(pieces[step - 1], PLANE, line_pairs(False, step)) for step in (1, 3, 2)]
    grad = sum_rows(keep, got)
    own = [kept(step, grad) for step in range(4)]
    grad = lax.all_to_all(grad, "z", 0, 0, tiled=True)
    state, *own = lax.optimization_barrier((state, *own))
    copies, made = adam(grad, state, hadamard_table())

    slab = lax.all_to_all(copies, "z", 0, 0, tiled=True)
    slab = stacked(slab, made)
    got = {step: lax.ppermute(slab, PLANE, line_pairs(False, step)) for step in (1, 3, 2)}
    parts = [slab, got[3], got[2], got[1]]
    upper, lower, made = join(parts, q, lax.axis_index("z"), both_cores(*got.values()))
    upper, lower = upper.reshape(1152, 256), lower.reshape(1152, 256)
    left_upper, right_lower = pass_on(upper, 1), pass_on(lower, 3)
    left_lower, right_upper = pass_on(lower, 1), pass_on(upper, 3)

    out = outputs_chunk(own[0], other[0], upper, lower, None)
    made = lax.ppermute(made, PLANE, [(a, b) for a, b, _ in home])
    upper, lower = pass_on(left_upper, 1), pass_on(right_lower, 3)
    out = outputs_chunk(own[3], other[3], left_upper, left_lower, out)
    out = outputs_chunk(own[1], other[1], right_upper, right_lower, out)
    out = outputs_chunk(own[2], other[2], upper, lower, out)
    weight_new, code_new, second_new, scale_new = unpack(made)
    outputs = (out[:256] + lax.ppermute(out[256:], "c", SWAP)).astype(BF)
    rows = lambda a: a.reshape(288, a.shape[2])
    return (outputs, rows(weight_new), rows(code_new), rows(scale_new), rows(second_new))


def solution(mesh):
    split = Mesh(mesh.devices.reshape(2, 2, 2, 4, 8), AXES)
    tokens = P(AXES, None)
    shard = P(("xh", "y", "z"), None)
    return jax.shard_map(
        per_device,
        mesh=split,
        in_specs=(tokens, tokens, shard, shard, shard, shard),
        out_specs=(tokens, shard, shard, shard, shard),
        check_vma=False,
    )
```

```python
import itertools
import math

import jax
import jax.numpy as jnp
from jax import lax
from jax.experimental import pallas as pl
from jax.experimental.pallas import tpu as pltpu
from jax.sharding import Mesh, PartitionSpec as P

AXES = ("xl", "c", "xh", "y", "z")
PLANE = ("xl", "c", "xh", "y")
BF = jnp.bfloat16
F32 = jnp.float32
SWAP = [(0, 1), (1, 0)]


def flat(x, c, y):
    return ((x % 2 * 2 + c) * 2 + x // 2) * 4 + y


def line_pairs(first, step):
    pairs = []
    for x in range(4):
        for c in range(2):
            for y in range(4):
                along_x = (c == 0) == first
                to = flat((x + step) % 4, c, y) if along_x else flat(x, c, (y + step) % 4)
                pairs.append((flat(x, c, y), to))
    return pairs


def home_pairs():
    pairs = []
    for c in range(2):
        for p in range(4):
            owners = [(p, c, q) if c == 0 else (q, c, p) for q in range(4)]
            holders = [(2 * c + i, core, p) for i in range(2) for core in range(2)]

            def hops(order):
                apart = lambda a, b: min((a - b) % 4, (b - a) % 4)
                pair = zip(owners, order)
                each = [apart(o[0], h[0]) + apart(o[2], h[2]) + (0.1 if o[1] != h[1] else 0) for o, h in pair]
                return sum(each) + 0.01 * max(each)

            best = min(itertools.permutations(holders), key=hops)
            pairs += [(flat(*owners[q]), flat(*best[q]), q) for q in range(4)]
    return pairs


def hadamard_table():
    index = jnp.arange(128, dtype=jnp.int32)
    parity = jnp.zeros((128, 128), jnp.int32)
    for level in range(7):
        left = jnp.bitwise_and(jnp.right_shift(index, level), 1)
        parity = parity + left[:, None] * left[None, :]
    signs = 1 - 2 * jnp.bitwise_and(parity, 1)
    return signs.astype(F32) / math.sqrt(128.0)


def call(kernel, out_shape, scratch=(), in_specs=None, grid=()):
    options = {} if in_specs is None else {"in_specs": in_specs}
    return pl.pallas_call(
        kernel,
        out_shape=out_shape,
        scratch_shapes=scratch,
        grid=grid,
        compiler_params=pltpu.CompilerParams(vmem_limit_bytes=16 << 20),
        cost_estimate=pl.CostEstimate(flops=1000, bytes_accessed=1000, transcendentals=0),
        **options,
    )


def shaped(shape, dtype):
    return jax.ShapeDtypeStruct(shape, dtype)


def after(value, *others):
    return lax.optimization_barrier((value, *others))[0]


SCALAR = pl.BlockSpec(memory_space=pltpu.SMEM)
VMEM = pl.BlockSpec(memory_space=pltpu.VMEM)
ANY = pl.BlockSpec(memory_space=pl.ANY)


def gradient_rows(own, other, cot_own, cot_other, rows, dtype, added=(), behind=()):
    contract = (((0,), (0,)), ((), ()))
    size = rows.stop - rows.start

    def kernel(own_ref, other_ref, cot_own_ref, cot_other_ref, *refs):
        for i in range(0, size, 384):
            part = pl.ds(i, 384)
            term = lax.dot_general(own_ref[:, part], cot_own_ref[...], contract, preferred_element_type=F32)
            term += lax.dot_general(other_ref[:, part], cot_other_ref[...], contract, preferred_element_type=F32)
            for ref in refs[: len(added)]:
                term += ref[pl.ds(i, 384), :].astype(F32)
            refs[-1][pl.ds(i, 384), :] = term.astype(dtype)

    columns = pl.BlockSpec((256, size), lambda i: (0, rows.start // size))
    specs = [columns] * 2 + [VMEM] * (2 + len(added)) + [ANY] * len(behind)
    return call(kernel, shaped((size, 256), dtype), (), specs, (1,))(own, other, cot_own, cot_other, *added, *behind)


def sum_and_split(total, upper, lower, q):
    def kernel(q_ref, total_ref, a_ref, b_ref, d_ref, e_ref, keep_ref, one_ref, two_ref, three_ref, value_ref):
        for z in range(8):
            rows, local = pl.ds(z * 288, 288), pl.ds(z % 4 * 288, 288)
            f_ref, g_ref = (a_ref, b_ref) if z < 4 else (d_ref, e_ref)
            value_ref[rows, :] = total_ref[rows, :] + f_ref[local, :].astype(F32) + g_ref[local, :].astype(F32)
            for step, ref in enumerate((keep_ref, one_ref, two_ref, three_ref)):
                at = pl.multiple_of(z * 288 + (q_ref[0] + step) % 4 * 72, 8)
                ref[z] = value_ref[pl.ds(at, 72), :].astype(ref.dtype)

    return call(
        kernel,
        [shaped((8, 72, 256), F32)] + [shaped((8, 72, 256), BF)] * 3,
        [pltpu.VMEM((2304, 256), F32)],
        [SCALAR] + [VMEM] * 5,
    )(q.reshape(1), total, *upper, *lower)


def sum_rows(keep, terms):
    def kernel(keep_ref, a_ref, b_ref, d_ref, out_ref):
        out_ref[...] = (
            keep_ref[...] + a_ref[...].astype(F32) + b_ref[...].astype(F32) + d_ref[...].astype(F32)
        ).astype(BF)

    return call(kernel, shaped((8, 72, 256), BF))(keep, *terms)


def adam(terms, state, table):
    def kernel(terms_ref, state_ref, table_ref, copies_ref, made_ref):
        grad = terms_ref[0].astype(F32)
        for z in range(1, 8):
            grad += terms_ref[z].astype(F32)
        grad *= 1.0 / 256.0
        table = table_ref[...]

        def rotate(block):
            return jnp.dot(block, table, precision=lax.Precision.HIGHEST, preferred_element_type=F32)

        second = 0.95 * state_ref[2].astype(F32) + 0.05 * grad * grad
        code = state_ref[1].astype(F32)
        weight = state_ref[0].astype(F32)
        scale = state_ref[3].astype(F32)
        scales = []
        for block in range(2):
            at = slice(128 * block, 128 * block + 128)
            first_old = rotate(code[:, at] * scale[:, block : block + 1])
            first = 0.9 * first_old + 0.1 * grad[:, at]
            weight_new = (weight[:, at] - 0.002 * first / (jnp.sqrt(second[:, at]) + 1e-08)).astype(BF)
            for z in range(8):
                copies_ref[z, :, at] = weight_new
            rotated = rotate(first)
            scales.append(jnp.max(jnp.abs(rotated), axis=1, keepdims=True).astype(BF).astype(F32))
            made_ref[0, :, at] = (rotated / (scales[block] + 1e-06)).astype(BF)
        made_ref[1] = second.astype(BF)
        column = lax.broadcasted_iota(jnp.int32, (72, 256), 1)
        made_ref[2] = jnp.where(column % 2 == 0, scales[0], scales[1]).astype(BF)

    return call(kernel, [shaped((8, 72, 256), BF), shaped((3, 72, 256), BF)])(terms, state, table)


def stacked(slab, made):
    def kernel(slab_ref, made_ref, out_ref):
        out_ref[:8] = slab_ref[...]
        out_ref[8:] = made_ref[...]

    return call(kernel, shaped((11, 72, 256), BF))(slab, made)


def both_cores(*arrays):
    def kernel(*refs):
        refs[-1][...] = jnp.zeros((16, 128), BF)

    return lax.ppermute(call(kernel, shaped((16, 128), BF), (), [ANY] * len(arrays))(*arrays), "c", SWAP)


def join(parts, q, z, ready):
    def kernel(place_ref, a_ref, b_ref, d_ref, e_ref, ready_ref, upper_ref, lower_ref, home_ref):
        column = lax.broadcasted_iota(jnp.int32, (72, 256), 1)
        scales = jnp.zeros((72, 256), F32)
        for step, ref in enumerate((a_ref, b_ref, d_ref, e_ref)):
            quarter = (place_ref[0] + step) % 4
            upper_ref[:, quarter] = ref[:4]
            lower_ref[:, quarter] = ref[4:8]
            home_ref[quarter] = ref[place_ref[1]]
            home_ref[4 + quarter] = ref[8]
            home_ref[8 + quarter] = ref[9]
            scales = jnp.where(column // 2 == quarter, ref[10].astype(F32), scales)
        home_ref[12] = scales.astype(BF)

    return call(
        kernel,
        [shaped((4, 4, 72, 256), BF)] * 2 + [shaped((13, 72, 256), BF)],
        (),
        [SCALAR] + [VMEM] * 4 + [ANY],
    )(jnp.stack([q, z]), *parts, ready)


def unpack(home):
    def kernel(home_ref, weight_ref, code_ref, second_ref, scale_ref):
        weight_ref[...] = home_ref[:4]
        code_ref[...] = home_ref[4:8]
        second_ref[...] = home_ref[8:12]
        for quarter in range(4):
            scale_ref[quarter] = home_ref[12][:, 2 * quarter : 2 * quarter + 2]

    return call(kernel, [shaped((4, 72, 256), BF)] * 3 + [shaped((4, 72, 2), BF)])(home)


def outputs_chunk(own, other, upper, lower, total):
    def kernel(own_ref, other_ref, upper_ref, lower_ref, *refs):
        for half, ref in ((slice(0, 256), own_ref), (slice(256, 512), other_ref)):
            value = jnp.dot(ref[:, :1152], upper_ref[...], preferred_element_type=F32)
            value += jnp.dot(ref[:, 1152:], lower_ref[...], preferred_element_type=F32)
            refs[-1][half] = value if total is None else refs[0][half] + value

    given = [] if total is None else [total]
    return call(kernel, shaped((512, 256), F32))(own, other, upper, lower, *given)


def per_device(tokens, cotangent, weight, code, scale, second_old):
    xl = lax.axis_index("xl")
    c = lax.axis_index("c")
    x = lax.axis_index("xh") * 2 + xl
    y = lax.axis_index("y")
    p = jnp.where(c == 0, x, y)
    q = jnp.where(c == 0, y, x)

    home = home_pairs()

    def taken(place, *behind):
        return lax.dynamic_slice(tokens, (0, after(place, *behind) * 2304), (256, 2304))

    def sent(step, *behind):
        return taken((1 - c) * 4 + (q + step) % 4, *behind)

    def kept(step, *behind):
        return taken(c * 4 + (p + step) % 4, *behind)

    def swap(chunk):
        return lax.ppermute(chunk, "c", SWAP)

    def pass_on(rows, step):
        return lax.ppermute(rows, PLANE, line_pairs(True, step))

    def rows_of(step, rows, *added, dtype=BF, behind=()):
        return gradient_rows(own[step], other[step], cotangent, cot_other, rows, dtype, added, behind)

    upper, lower, both = slice(0, 1152), slice(1152, 2304), slice(0, 2304)
    own, other = {}, {}
    cot_other = swap(cotangent)
    chunk = sent(2)
    other[2] = swap(after(chunk, cot_other))
    words = [0] * 4
    for _, holder, which in home:
        words[holder // 8] += which << (holder % 8 * 2)
    word = jnp.where(xl == 0, jnp.where(c == 0, words[0], words[1]), jnp.where(c == 0, words[2], words[3]))
    at = lax.shift_right_logical(word, 2 * (lax.axis_index("xh") * 4 + y)) % 4
    at = after(at, chunk) * 72
    state = [weight, code, second_old, jnp.pad(scale, ((0, 0), (0, 254)))]
    state = jnp.stack([lax.dynamic_slice(a, (at, 0), (72, 256)) for a in state])
    state = lax.ppermute(state, PLANE, [(b, a) for a, b, _ in home])
    taken_here = [kept(step, chunk) for step in (2, 1, 3, 0)]
    taken_there = [sent(step, chunk) for step in (1, 3, 0)]
    *taken_here, one, three, zero = lax.optimization_barrier((*taken_here, *taken_there))
    own = dict(zip((2, 1, 3, 0), taken_here))
    other[1], other[3], other[0] = swap(one), swap(three), swap(zero)
    from_left, from_right = pass_on(rows_of(2, upper), 1), pass_on(rows_of(2, lower), 3)
    left_lower = pass_on(rows_of(1, lower), 1)
    right_upper = pass_on(rows_of(3, upper), 3)
    left_upper = pass_on(rows_of(1, upper, from_left), 1)
    right_lower = pass_on(rows_of(3, lower, from_right), 3)
    total = rows_of(0, both, dtype=F32, behind=(state,))

    keep, *pieces = sum_and_split(total, (left_upper, right_upper), (left_lower, right_lower), q)
    got = [lax.ppermute(pieces[step - 1], PLANE, line_pairs(False, step)) for step in (1, 3, 2)]
    grad = sum_rows(keep, got)
    own = [kept(step, grad) for step in range(4)]
    grad = lax.all_to_all(grad, "z", 0, 0, tiled=True)
    state, *own = lax.optimization_barrier((state, *own))
    copies, made = adam(grad, state, hadamard_table())

    slab = lax.all_to_all(copies, "z", 0, 0, tiled=True)
    slab = stacked(slab, made)
    got = {step: lax.ppermute(slab, PLANE, line_pairs(False, step)) for step in (1, 3, 2)}
    parts = [slab, got[3], got[2], got[1]]
    upper, lower, made = join(parts, q, lax.axis_index("z"), both_cores(*got.values()))
    upper, lower = upper.reshape(1152, 256), lower.reshape(1152, 256)
    left_upper, right_lower = pass_on(upper, 1), pass_on(lower, 3)
    left_lower, right_upper = pass_on(lower, 1), pass_on(upper, 3)

    out = outputs_chunk(own[0], other[0], upper, lower, None)
    made = lax.ppermute(made, PLANE, [(a, b) for a, b, _ in home])
    upper, lower = pass_on(left_upper, 1), pass_on(right_lower, 3)
    out = outputs_chunk(own[3], other[3], left_upper, left_lower, out)
    out = outputs_chunk(own[1], other[1], right_upper, right_lower, out)
    out = outputs_chunk(own[2], other[2], upper, lower, out)
    weight_new, code_new, second_new, scale_new = unpack(made)
    outputs = (out[:256] + lax.ppermute(out[256:], "c", SWAP)).astype(BF)
    rows = lambda a: a.reshape(288, a.shape[2])
    return (outputs, rows(weight_new), rows(code_new), rows(scale_new), rows(second_new))


def solution(mesh):
    split = Mesh(mesh.devices.reshape(2, 2, 2, 4, 8), AXES)
    tokens = P(AXES, None)
    shard = P(("xh", "y", "z"), None)
    return jax.shard_map(
        per_device,
        mesh=split,
        in_specs=(tokens, tokens, shard, shard, shard, shard),
        out_specs=(tokens, shard, shard, shard, shard),
        check_vma=False,
    )
```
